32 devices in a mesh: groups: 2 (over y), inst: 4 (over z), tp: 4 (over x, core).
Axes of the slice: x: 2, y: 2, z: 4, core: 2. Of those that a mesh axis runs over, the one named last changes fastest.
Arguments:
- kv_pool: bfloat16 [512, 2, 8, 32, 128], P(('groups', 'inst'), None, 'tp'), parts along dimension 0, may hold values from -6 to 6
- page_table: int32 [128, 4], P(('groups', 'inst')), parts along dimension 0, may hold values from 0 to 63, as said below
- lengths: int32 [128], P(('groups', 'inst')), parts along dimension 0, may hold values from 1 to 126
- partner: int32 [128], P(('groups', 'inst')), parts along dimension 0, may hold values from 0 to 63, as said below
- queries: bfloat16 [128, 2, 32, 128], P(('groups', 'inst'), None, 'tp'), parts along dimension 0, may hold values from -150 to 150
- new_kv: bfloat16 [128, 2, 2, 8, 128], P(('groups', 'inst'), None, None, 'tp'), parts along dimension 0, may hold values from -6 to 6
- out_weight: bfloat16 [4096, 2560], P('tp'), may hold values from -0.25 to 0.25
Outputs:
- layer_out: bfloat16 [128, 2, 2560], P(('groups', 'inst', 'tp')), parts along dimension 0
- new_cache: bfloat16 [128, 2, 8, 128, 128], P(('groups', 'inst'), None, 'tp'), parts along dimension 0
The draws below stay inside these ranges and needn't reach their ends.
There are 2 independent parts, one for each index of `groups`. The reference program is written for one: setup_inputs(seed, part) draws one part's arguments, and reference() takes and returns one part's arrays. A program takes and returns all parts, laid end to end along the dimension named above; an argument that names none is the same for every part. Nothing has to cross between parts.
Inputs may be any that keep to these rules, and one draw needn't show every extreme that they name: `page_table`: each instance's rows name distinct pages of its own pool of 64; only the first ceil(lengths / 32) entries of a row are read. Requests trade slots in pairs: partner is its own inverse. At most one request goes from one instance to another.
All inputs are finite; a program needn't handle non-finite values.
Results may differ from the reference program's by a relative error of at most 0.0059.
Values may be sent and summed in bfloat16 or wider, within the bound.
A program may use at most 64 MiB of HBM per device.

```python
import math
import jax
import jax.numpy as jnp
from jax import lax

HD = 128
KVH = 8
QPK = 4
DW = 2560
PAGE = 32
MAXP = 4
STEPS = 2
REQ_DEV = 16
INSTANCES = 4
QH = 32
PAGES = 64
REQS = 64


def layout(key):
    key_rank, key_slots, key_long, key_short, key_pages = jax.random.split(key, 5)
    half = INSTANCES // 2
    ranking = jax.random.permutation(key_rank, INSTANCES).astype(jnp.int32)
    standing = jnp.argsort(ranking).astype(jnp.int32)[:, None]
    slot_order = jax.vmap(lambda sub: jax.random.permutation(sub, REQ_DEV))(jax.random.split(key_slots, INSTANCES)).astype(jnp.int32)
    position = jnp.argsort(slot_order, axis=1).astype(jnp.int32)
    instance = jnp.arange(INSTANCES, dtype=jnp.int32)[:, None]
    slot_index = jnp.arange(REQ_DEV, dtype=jnp.int32)[None, :]
    is_hot = standing < half
    moving = position < half
    other_pos = jnp.mod(-position, half)
    cold_rank = jnp.mod(standing + position, half)
    cold_inst = ranking[jnp.clip(half + cold_rank, 0, INSTANCES - 1)]
    cold_slot = slot_order[cold_inst, jnp.clip(other_pos, 0, REQ_DEV - 1)]
    hot_rank = jnp.mod(standing - half + position, half)
    hot_inst = ranking[jnp.clip(hot_rank, 0, INSTANCES - 1)]
    hot_slot = slot_order[hot_inst, jnp.clip(other_pos, 0, REQ_DEV - 1)]
    stay_slot = instance * REQ_DEV + slot_index
    sending = is_hot & moving
    getting = jnp.logical_not(is_hot) & moving
    partner = jnp.where(sending, cold_inst * REQ_DEV + cold_slot, jnp.where(getting, hot_inst * REQ_DEV + hot_slot, stay_slot))
    long_len = jax.random.randint(key_long, (INSTANCES, REQ_DEV), (MAXP - 1) * PAGE + 1, MAXP * PAGE - 1)
    long_len = jnp.where(position == REQ_DEV - 1, MAXP * PAGE - 2, long_len)
    short_len = jax.random.randint(key_short, (INSTANCES, REQ_DEV), 1, PAGE - 1)
    lengths = jnp.where(is_hot, long_len, short_len).astype(jnp.int32)
    pool_order = jax.vmap(lambda sub: jax.random.permutation(sub, PAGES))(jax.random.split(key_pages, INSTANCES))
    return (partner.reshape(REQS).astype(jnp.int32), lengths.reshape(REQS), pool_order.reshape(REQS, MAXP).astype(jnp.int32))


def draw_partner(key, part):
    return layout(key)[0]


def draw_lengths(key, part):
    return layout(key)[1]


def draw_page_table(key, part):
    return layout(key)[2]


def draw_queries(key, part):
    key = jax.random.fold_in(key, 11)
    key_values = jax.random.fold_in(key, 0)
    shape = (REQS, STEPS, QH, HD)
    return jax.random.truncated_normal(key_values, -6.0, 6.0, shape, jnp.float32).astype(jnp.bfloat16)


def block_levels(stream_key, shape, shards, smallest, top_value):
    gain = 1.0
    for axis_at, blocks in shards:
        heights = jax.random.uniform(jax.random.fold_in(jax.random.fold_in(stream_key, 6), axis_at), (blocks,), jnp.float32, smallest / len(shards), top_value / len(shards))
        gain = gain * jnp.repeat(jnp.exp(heights), shape[axis_at] // blocks).reshape((-1,) + (1,) * (len(shape) - 1 - axis_at))
    return gain


def noise(own_key, shape, spread, reach, shards=(), kind=jnp.bfloat16):
    drawn = jax.random.normal(own_key, shape, jnp.float32) * spread
    if len(shards) > 0:
        drawn = block_levels(own_key, shape, shards, -0.22, 0.18) * drawn
    return jnp.clip(drawn, min=-reach, max=reach).astype(kind)


def setup_inputs(seed: int = 0, part: int = 0) -> dict:
    splits = jax.random.split(jax.random.key(seed), 8)
    part_keys = jax.random.split(jax.random.fold_in(splits[7], part), 8)
    kv_pool = noise(part_keys[0], (INSTANCES * PAGES, 2, KVH, PAGE, HD), 1.0, 6.0, ((0, 4), (2, 4)))
    page_table = draw_page_table(jax.random.fold_in(jax.random.fold_in(splits[7], part), 71), part)
    lengths = draw_lengths(jax.random.fold_in(jax.random.fold_in(splits[7], part), 71), part)
    partner = draw_partner(jax.random.fold_in(jax.random.fold_in(splits[7], part), 71), part)
    queries = draw_queries(jax.random.fold_in(jax.random.fold_in(splits[7], part), 71), part)
    new_kv = noise(part_keys[5], (REQS, STEPS, 2, KVH, HD), 1.0, 6.0, ((0, 4), (3, 4)))
    out_weight = noise(splits[6], (QH * HD, DW), (QPK * HD) ** -0.5, 0.25, ((0, 4),))
    return dict(kv_pool=kv_pool, page_table=page_table, lengths=lengths, partner=partner, queries=queries, new_kv=new_kv, out_weight=out_weight)


def reference(kv_pool, page_table, lengths, partner, queries, new_kv, out_weight):
    span = MAXP * PAGE
    owner = jnp.arange(REQS, dtype=jnp.int32) // REQ_DEV
    global_pages = page_table + (owner * PAGES)[:, None]
    page_rows = kv_pool[global_pages]
    cached = page_rows.transpose(0, 2, 3, 1, 4, 5).reshape(REQS, 2, KVH, span, HD)
    position = jnp.arange(span, dtype=jnp.int32)
    inside = position[None, :] < lengths[:, None]
    cached = jnp.where(inside[:, None, None, :, None], cached, jnp.zeros((), cached.dtype))
    moved = cached[partner]
    moved_len = lengths[partner]
    for step in range(STEPS):
        landing = position[None, :] == (moved_len + step)[:, None]
        moved = jnp.where(landing[:, None, None, :, None], new_kv[:, step][:, :, :, None, :], moved)
    new_cache = moved
    grouped = queries.astype(jnp.float32).reshape(REQS, STEPS, KVH, QPK, HD)
    key_rows = new_cache[:, 0].astype(jnp.float32)
    value_rows = new_cache[:, 1].astype(jnp.float32)
    scores = jnp.einsum('ntgqd,ngpd->ntgqp', grouped, key_rows, precision=lax.Precision.HIGHEST) / math.sqrt(HD)
    limit = moved_len[:, None] + jnp.arange(STEPS, dtype=jnp.int32)[None, :] + 1
    visible = position[None, None, :] < limit[:, :, None]
    scores = jnp.where(visible[:, :, None, None, :], scores, jnp.float32(-1e+30))
    largest = lax.optimization_barrier(jnp.max(scores, axis=-1, keepdims=True))
    expo = jnp.exp(scores - largest)
    weights = (expo / lax.optimization_barrier(jnp.sum(expo, axis=-1, keepdims=True))).astype(jnp.bfloat16)
    attended = jnp.einsum('ntgqp,ngpd->ntgqd', weights.astype(jnp.float32), value_rows, precision=lax.Precision.HIGHEST)
    attended = attended.astype(jnp.bfloat16).reshape(REQS * STEPS, QH * HD)
    layer_out = jnp.dot(attended, out_weight, preferred_element_type=jnp.float32)
    layer_out = layer_out.astype(jnp.bfloat16).reshape(REQS, STEPS, DW)
    return (layer_out, new_cache)
```

```python
import functools

import jax
import jax.numpy as jnp
from jax import lax
from jax.experimental import pallas as pl
from jax.experimental.pallas import tpu as pltpu
from jax.sharding import PartitionSpec as P

MESH = pl.DeviceIdType.MESH
BF16 = jnp.bfloat16
F32 = jnp.float32
WIDE = 512


def move_kernel(
    dims, pt, ln, pr, q_ref, nk_ref, pool_hbm, w_hbm, loc_hbm, arr_hbm, lo_ref,
    poolv, wv, qn, qbox, qarr, obox, locv, att, abox, aarr, merged, flat, prodf, pbox, parr,
    dma_sem, loc_sem, q_send, q_recv, p_send, p_recv, a_send, a_recv, r_send, r_recv,
):
    n, tp, slots, steps, heads, groups, pages, page, span, hd, features = dims
    rows = steps * heads
    new_at = -(-rows // 16) * 16
    per = heads // groups
    body = 2 * groups * span
    me = lax.axis_index("inst")
    col = lax.axis_index("tp")
    own = slots // tp * steps
    fold = max(1, 16 // own)
    narrow = WIDE // fold
    chunks = features // WIDE

    pool_copy = pltpu.make_async_copy(pool_hbm, poolv, dma_sem.at[0])
    pool_copy.start()
    w_copy = pltpu.make_async_copy(w_hbm, wv, dma_sem.at[1])
    w_copy.start()

    barrier = pltpu.get_barrier_semaphore()
    for k in range(1, n):
        pl.semaphore_signal(
            barrier, inc=1, device_id={"inst": lax.rem(me + k, n)}, device_id_type=MESH
        )
    for i in range(1, tp):
        pl.semaphore_signal(
            barrier, inc=1, device_id={"tp": lax.rem(col + i, tp)}, device_id_type=MESH
        )

    def pack(j, carry):
        parts = [q_ref[j, t].astype(F32) for t in range(steps)]
        if new_at > rows:
            parts.append(jnp.zeros((new_at - rows, hd), F32))
        parts += [nk_ref[j, t, c].astype(F32) for t in range(steps) for c in range(2)]
        fill = qn.shape[1] - new_at - steps * 2 * groups
        parts.append(jnp.zeros((fill, hd), F32))
        qn[j] = jnp.concatenate(parts, axis=0).astype(BF16)
        return carry

    lax.fori_loop(0, slots, pack, 0)

    def slot_for(k):
        other = lax.rem(me + k, n)
        found = jnp.int32(0)
        for j in range(slots):
            found = jnp.where(pr[j] // slots == other, jnp.int32(j), found)
        return found

    def build_q(k, carry):
        qbox[k] = qn[slot_for(k)]
        return carry

    lax.fori_loop(1, n, build_q, 0)
    aarr[0] = jnp.zeros(aarr.shape[1:], BF16)
    pl.semaphore_wait(barrier, n - 1 + tp - 1)

    def remote(src, dst, send, recv, where):
        return pltpu.make_async_remote_copy(
            src_ref=src, dst_ref=dst, send_sem=send, recv_sem=recv,
            device_id=where, device_id_type=MESH,
        )

    def q_copy(k):
        return remote(qbox.at[k], qarr.at[k], q_send.at[k], q_recv.at[k],
                      {"inst": lax.rem(me + k, n)})

    def p_copy(k):
        return remote(obox.at[k], arr_hbm.at[k], p_send.at[k], p_recv.at[k],
                      {"inst": lax.rem(me + k, n)})

    def a_copy(k):
        return remote(abox.at[k], aarr.at[k], a_send.at[k], a_recv.at[k],
                      {"inst": lax.rem(me + k, n)})

    order = sorted(range(1, n), key=lambda k: abs(k - n // 2))
    for k in order:
        q_copy(k).start()
    pool_copy.wait()

    row_at = lax.broadcasted_iota(jnp.int32, (page, hd), 0)

    def stored(slot, known):
        for m in range(pages):
            at = row_at + page * m
            inside = at < known
            where = pt[slot, m]
            for c in range(2):
                for g in range(groups):
                    x = poolv[where, c, g].astype(F32)
                    yield m, c, g, at, jnp.where(inside, x, 0.0)

    def place(m, c, g):
        return pl.ds((c * groups + g) * span + page * m, page)

    def build_pages(k):
        slot = slot_for(k)
        known = ln[slot]
        for m, c, g, _, x in stored(slot, known):
            obox[k, place(m, c, g), :] = x.astype(BF16)
        obox[k, pl.ds(body, 16), :] = jnp.full((16, hd), known.astype(F32), F32).astype(BF16)

    for k in order:
        build_pages(k)
        p_copy(k).start()

    def fresh_rows(packed):
        extra = packed[new_at:].astype(F32)
        return lambda t, c, g: extra[(t * 2 + c) * groups + g:(t * 2 + c) * groups + g + 1]

    r_at = lax.broadcasted_iota(jnp.int32, (rows, groups * span), 0)
    c_at = lax.broadcasted_iota(jnp.int32, (rows, groups * span), 1)
    same = (r_at % heads) // per == c_at // span
    ahead = c_at % span - r_at // heads

    def attend(asked, keys, values, known):
        scores = lax.dot_general(
            asked, keys, (((1,), (1,)), ((), ())), preferred_element_type=F32
        ) * (hd ** -0.5)
        scores = jnp.where(same & (ahead <= known), scores, -1e30)
        expo = jnp.exp(scores - jnp.max(scores, axis=-1, keepdims=True))
        weights = (expo / jnp.sum(expo, axis=-1, keepdims=True)).astype(BF16)
        return jnp.dot(weights, values, preferred_element_type=F32)

    def finish(slot, known, packed, dst, j):
        new = fresh_rows(packed)
        for m, c, g, at, x in stored(slot, known):
            for t in range(steps):
                x = jnp.where(at == known + t, new(t, c, g), x)
            dst[j, place(m, c, g), :] = x.astype(BF16)

    half = groups * span
    extra = slots

    def leaver(k):
        slot = slot_for(k)
        known = ln[slot]
        packed = qarr[n - k]
        finish(slot, known, packed, locv, extra)
        out = attend(packed[:rows], locv[extra, pl.ds(0, half), :],
                     locv[extra, pl.ds(half, half), :], known)
        if rows < 16:
            out = jnp.concatenate([out, jnp.zeros((16 - rows, hd), F32)], axis=0)
        abox[k] = out.astype(BF16)

    for k in order:
        q_copy(n - k).wait_recv()
        leaver(k)
        a_copy(k).start()

    def stay(j, carry):
        slot = pr[j] % slots
        known = ln[slot]
        packed = qn[j]
        finish(slot, known, packed, locv, j)
        pltpu.make_async_copy(locv.at[j], loc_hbm.at[j], loc_sem.at[j]).start()
        att[j] = attend(packed[:rows], locv[j, pl.ds(0, half), :],
                        locv[j, pl.ds(half, half), :], known)
        return carry

    lax.fori_loop(0, slots, stay, 0, unroll=4)

    for k in order:
        a_copy(k).wait_recv()
    for j in range(slots):
        back = lax.rem(me - pr[j] // slots + n, n)
        got = aarr[back].astype(F32)[:rows]
        merged[pl.ds(j * rows, rows), :] = jnp.where(back == 0, att[j], got)
    for h in range(heads):
        flat[:, pl.ds(h * hd, hd)] = merged[
            pl.ds(h, slots * steps, stride=heads), :
        ].astype(BF16)
    w_copy.wait()

    def r_copy(c, i):
        return remote(pbox.at[c, lax.rem(col + i, tp)], parr.at[c, i], r_send.at[c, i],
                      r_recv.at[c, i], {"tp": lax.rem(col + i, tp)})

    for c in range(chunks):
        prod = jnp.dot(flat[...], wv[:, pl.ds(c * WIDE, WIDE)], preferred_element_type=F32)
        for d in range(tp):
            mine = prod[d * own:(d + 1) * own]
            prodf[c, d] = mine
            pbox[c, d] = jnp.concatenate(
                [mine[:, f * narrow:(f + 1) * narrow] for f in range(fold)], axis=0
            ).astype(BF16)
        for i in range(1, tp):
            r_copy(c, i).start()
    for c in range(chunks):
        total = prodf[c, col]
        for i in range(1, tp):
            r_copy(c, i).wait_recv()
            part = parr[c, i].astype(F32)
            total += jnp.concatenate(
                [part[f * own:(f + 1) * own] for f in range(fold)], axis=1
            )
        for r in range(own // steps):
            lo_ref[r, :, pl.ds(c * WIDE, WIDE)] = total[r * steps:(r + 1) * steps].astype(BF16)

    for c in range(chunks):
        for i in range(1, tp):
            r_copy(c, i).wait_send()
    for k in order:
        q_copy(k).wait_send()
        a_copy(k).wait_send()
    for j in range(slots):
        pltpu.make_async_copy(locv.at[j], loc_hbm.at[j], loc_sem.at[j]).wait()
    for k in order:
        p_copy(k).wait_send()
        p_copy(k).wait_recv()


def place_kernel(dims, pr, nk_ref, loc_hbm, arr_hbm, lo_in, new_hbm, lo_out, vbuf, sem, in_sem):
    n, tp, slots, steps, heads, groups, pages, page, span, hd, features = dims
    body = 2 * groups * span
    me = lax.axis_index("inst")
    lo_copy = pltpu.make_async_copy(lo_in, lo_out, sem.at[slots])
    lo_copy.start()

    def source(j):
        return lax.rem(me - pr[j] // slots + n, n)

    def fetch(j):
        return pltpu.make_async_copy(arr_hbm.at[source(j)], vbuf.at[source(j)], in_sem.at[j])

    def keep(j):
        return pltpu.make_async_copy(loc_hbm.at[j], new_hbm.at[j], sem.at[j])

    def put(j):
        return pltpu.make_async_copy(vbuf.at[source(j), pl.ds(0, body)], new_hbm.at[j], sem.at[j])

    for j in range(slots):
        moved = source(j) != 0

        @pl.when(moved)
        def _():
            fetch(j).start()

        @pl.when(jnp.logical_not(moved))
        def _():
            keep(j).start()

    at = lax.broadcasted_iota(jnp.int32, (span, hd), 0)
    for j in range(slots):
        @pl.when(source(j) != 0)
        def _():
            fetch(j).wait()
            k = source(j)
            known = vbuf[k, pl.ds(body, 16), :].astype(F32)[:1].astype(jnp.int32)
            for c in range(2):
                rows = [nk_ref[j, t, c].astype(F32) for t in range(steps)]
                for g in range(groups):
                    where = pl.ds((c * groups + g) * span, span)
                    x = vbuf[k, where, :].astype(F32)
                    for t in range(steps):
                        x = jnp.where(at == known + t, rows[t][g:g + 1], x)
                    vbuf[k, where, :] = x.astype(BF16)
            put(j).start()

    for j in range(slots):
        keep(j).wait()
    lo_copy.wait()


def body(mesh, kv_pool, page_table, lengths, partner, queries, new_kv, out_weight):
    n, tp = mesh.shape["inst"], mesh.shape["tp"]
    slots, steps, heads, hd = queries.shape
    groups, page = kv_pool.shape[2], kv_pool.shape[3]
    pages = page_table.shape[1]
    features = out_weight.shape[1]
    span = pages * page
    dims = (n, tp, slots, steps, heads, groups, pages, page, span, hd, features)
    rows = steps * heads
    up = lambda x: -(-x // 16) * 16
    qrows = up(rows) + up(steps * 2 * groups)
    tokens = 2 * groups * span
    own = slots // tp * steps
    fold = max(1, 16 // own)
    chunks = features // WIDE
    vmem = pl.BlockSpec(memory_space=pltpu.VMEM)
    smem = pl.BlockSpec(memory_space=pltpu.SMEM)
    hbm = pl.BlockSpec(memory_space=pl.ANY)
    dma = pltpu.SemaphoreType.DMA
    loc, arr, lo = pl.pallas_call(
        functools.partial(move_kernel, dims),
        out_shape=(
            jax.ShapeDtypeStruct((slots, tokens, hd), BF16),
            jax.ShapeDtypeStruct((n, tokens + 16, hd), BF16),
            jax.ShapeDtypeStruct((slots // tp, steps, features), BF16),
        ),
        in_specs=[smem, smem, smem, vmem, vmem, hbm, hbm],
        out_specs=(hbm, hbm, vmem),
        scratch_shapes=[
            pltpu.VMEM(kv_pool.shape, BF16),
            pltpu.VMEM(out_weight.shape, BF16),
            pltpu.VMEM((slots, qrows, hd), BF16),
            pltpu.VMEM((n, qrows, hd), BF16),
            pltpu.VMEM((n, qrows, hd), BF16),
            pltpu.VMEM((n, tokens + 16, hd), BF16),
            pltpu.VMEM((slots + 1, tokens, hd), BF16),
            pltpu.VMEM((slots, rows, hd), F32),
            pltpu.VMEM((n, up(rows), hd), BF16),
            pltpu.VMEM((n, up(rows), hd), BF16),
            pltpu.VMEM((slots * rows, hd), F32),
            pltpu.VMEM((slots * steps, heads * hd), BF16),
            pltpu.VMEM((chunks, tp, own, WIDE), F32),
            pltpu.VMEM((chunks, tp, own * fold, WIDE // fold), BF16),
            pltpu.VMEM((chunks, tp, own * fold, WIDE // fold), BF16),
            dma((2,)), dma((slots,)),
            dma((n,)), dma((n,)), dma((n,)), dma((n,)), dma((n,)), dma((n,)),
            dma((chunks, tp)), dma((chunks, tp)),
        ],
        compiler_params=pltpu.CompilerParams(
            collective_id=0, has_side_effects=True, vmem_limit_bytes=28 << 20
        ),
        name="move",
    )(page_table, lengths, partner, queries, new_kv, kv_pool, out_weight)
    new_cache, layer_out = pl.pallas_call(
        functools.partial(place_kernel, dims),
        out_shape=(
            jax.ShapeDtypeStruct((slots, tokens, hd), BF16),
            jax.ShapeDtypeStruct(lo.shape, BF16),
        ),
        in_specs=[smem, vmem, hbm, hbm, hbm],
        out_specs=(hbm, hbm),
        scratch_shapes=[
            pltpu.VMEM((n, tokens + 16, hd), BF16),
            dma((slots + 1,)), dma((slots,)),
        ],
        compiler_params=pltpu.CompilerParams(vmem_limit_bytes=16 << 20),
        name="place",
    )(partner, new_kv, loc, arr, lo)
    return layer_out, new_cache.reshape(slots, 2, groups, span, hd)


def solution(mesh):
    in_specs = (
        P(("groups", "inst"), None, "tp", None, None),
        P(("groups", "inst"), None),
        P(("groups", "inst")),
        P(("groups", "inst")),
        P(("groups", "inst"), None, "tp", None),
        P(("groups", "inst"), None, None, "tp", None),
        P("tp", None),
    )
    out_specs = (
        P(("groups", "inst", "tp"), None, None),
        P(("groups", "inst"), None, "tp", None, None),
    )
    return jax.shard_map(
        functools.partial(body, mesh), mesh=mesh, in_specs=in_specs, out_specs=out_specs,
        check_vma=False,
    )
```

```python
import functools

import jax
import jax.numpy as jnp
from jax import lax
from jax.experimental import pallas as pl
from jax.experimental.pallas import tpu as pltpu
from jax.sharding import PartitionSpec as P

MESH = pl.DeviceIdType.MESH
BF16 = jnp.bfloat16
F32 = jnp.float32
WIDE = 512
FIRST = 3
EARLY = 0


def move_kernel(
    dims, pt_hbm, ln_hbm, pr_hbm, q_hbm, nk_hbm, pool_hbm, w_hbm, loc_hbm, arr_hbm, lo_ref,
    pt, ln, pr, q_ref, nk_ref, poolv, wv, qn, qbox, qarr, obox, lbox, locv, att, abox, aarr, merged, flat, prodf, pbox, parr,
    dma_sem, loc_sem, q_send, q_recv, p_send, p_recv, a_send, a_recv, r_send, r_recv,
):
    n, tp, slots, steps, heads, groups, pages, page, span, hd, features = dims
    rows = steps * heads
    new_at = -(-rows // 16) * 16
    per = heads // groups
    body = 2 * groups * span
    me = lax.axis_index("inst")
    col = lax.axis_index("tp")
    own = slots // tp * steps
    fold = max(1, 16 // own)
    narrow = WIDE // fold
    chunks = features // WIDE

    early = [
        pltpu.make_async_copy(src, dst, dma_sem.at[at])
        for at, (src, dst) in enumerate(
            [(pr_hbm, pr), (q_hbm, q_ref), (nk_hbm, nk_ref), (pt_hbm, pt), (ln_hbm, ln)]
        )
    ]
    for copy in early:
        copy.start()
    pool_copy = pltpu.make_async_copy(pool_hbm, poolv, dma_sem.at[5])
    pool_copy.start()
    w_copy = pltpu.make_async_copy(w_hbm, wv, dma_sem.at[6])

    barrier = pltpu.get_barrier_semaphore()
    for k in range(1, n):
        pl.semaphore_signal(
            barrier, inc=1, device_id={"inst": lax.rem(me + k, n)}, device_id_type=MESH
        )
    for i in range(1, tp):
        pl.semaphore_signal(
            barrier, inc=1, device_id={"tp": lax.rem(col + i, tp)}, device_id_type=MESH
        )

    for copy in early:
        copy.wait()
    aarr[0] = jnp.zeros(aarr.shape[1:], BF16)

    def slot_for(k):
        other = lax.rem(me + k, n)
        found = jnp.int32(0)
        for j in range(slots):
            found = jnp.where(pr[j] // slots == other, jnp.int32(j), found)
        return found

    def pack(j):
        parts = [q_ref[j, t].astype(F32) for t in range(steps)]
        if new_at > rows:
            parts.append(jnp.zeros((new_at - rows, hd), F32))
        parts += [nk_ref[j, t, c].astype(F32) for t in range(steps) for c in range(2)]
        fill = qn.shape[1] - new_at - steps * 2 * groups
        parts.append(jnp.zeros((fill, hd), F32))
        return jnp.concatenate(parts, axis=0).astype(BF16)

    order = sorted(range(1, n), key=lambda k: abs(k - n // 2))
    leaving = {k: slot_for(k) for k in order}
    for k in order:
        qbox[k] = pack(leaving[k])

    def remote(src, dst, send, recv, where):
        return pltpu.make_async_remote_copy(
            src_ref=src, dst_ref=dst, send_sem=send, recv_sem=recv,
            device_id=where, device_id_type=MESH,
        )

    def q_copy(k):
        return remote(qbox.at[k], qarr.at[k], q_send.at[k], q_recv.at[k],
                      {"inst": lax.rem(me + k, n)})

    cut = (body + 16) // FIRST // 16 * 16

    def p_copy(k, part):
        at = pl.ds(0, cut) if part == 0 else pl.ds(cut, body + 16 - cut)
        return remote(obox.at[k, at], arr_hbm.at[k, at], p_send.at[k, part],
                      p_recv.at[k, part], {"inst": lax.rem(me + k, n)})

    def a_copy(k):
        return remote(abox.at[k], aarr.at[k], a_send.at[k], a_recv.at[k],
                      {"inst": lax.rem(me + k, n)})

    row_at = lax.broadcasted_iota(jnp.int32, (page, hd), 0)

    def stored(slot, known):
        for m in range(pages):
            at = row_at + page * m
            inside = at < known
            where = pt[m, slot]
            for c in range(2):
                for g in range(groups):
                    x = poolv[where, c, g].astype(F32)
                    yield m, c, g, at, jnp.where(inside, x, 0.0)

    def place(m, c, g):
        return pl.ds((c * groups + g) * span + page * m, page)

    pl.semaphore_wait(barrier, n - 1 + tp - 1)
    for k in order:
        q_copy(k).start()
    pool_copy.wait()
    w_copy.start()
    for k in order:
        known = ln[leaving[k]]
        for m, c, g, _, x in stored(leaving[k], known):
            obox[k, place(m, c, g), :] = x.astype(BF16)
        obox[k, pl.ds(body, 16), :] = jnp.full((16, hd), known.astype(F32), F32).astype(BF16)
        p_copy(k, 0).start()

    r_at = lax.broadcasted_iota(jnp.int32, (rows, groups * span), 0)
    c_at = lax.broadcasted_iota(jnp.int32, (rows, groups * span), 1)
    same = (r_at % heads) // per == c_at // span
    ahead = c_at % span - r_at // heads
    reach = jnp.where(same, ahead, span * 2)
    half = groups * span

    def finish(slot, packed, dst, j):
        known = ln[slot]
        new = packed[new_at:].astype(F32)
        for m, c, g, at, x in stored(slot, known):
            for t in range(steps):
                r = (t * 2 + c) * groups + g
                x = jnp.where(at == known + t, new[r:r + 1], x)
            dst[j, place(m, c, g), :] = x.astype(BF16)

    def attend(asked, kept, knowns):
        scores = [
            jnp.where(
                reach <= known,
                lax.dot_general(
                    q, ref[at, pl.ds(0, half), :], (((1,), (1,)), ((), ())),
                    preferred_element_type=F32,
                ) * (hd ** -0.5),
                -1e30,
            )
            for q, (ref, at), known in zip(asked, kept, knowns)
        ]
        scores = jnp.concatenate(scores, axis=0)
        expo = jnp.exp(scores - jnp.max(scores, axis=-1, keepdims=True))
        weights = expo / jnp.sum(expo, axis=-1, keepdims=True)
        return [
            jnp.dot(weights[i * rows:(i + 1) * rows].astype(BF16),
                    ref[at, pl.ds(half, half), :], preferred_element_type=F32)
            for i, (ref, at) in enumerate(kept)
        ]

    def stays(low, high):
        def one(j, carry):
            packed = pack(j)
            qn[j] = packed
            finish(pr[j] % slots, packed, locv, j)
            pltpu.make_async_copy(locv.at[j], loc_hbm.at[j], loc_sem.at[j]).start()
            return carry

        lax.fori_loop(low, high, one, 0, unroll=2)
        js = range(low, high)
        outs = attend([qn[j, pl.ds(0, new_at), :][:rows] for j in js], [(locv, j) for j in js],
                      [ln[pr[j] % slots] for j in js])
        for j, out in zip(js, outs):
            att[j] = out

    early_slots = slots // EARLY if EARLY else 0
    if early_slots:
        stays(0, early_slots)
    for k in order:
        q_copy(n - k).wait_recv()
        finish(leaving[k], qarr[n - k], lbox, k)
    outs = attend([qarr[n - k, pl.ds(0, new_at), :][:rows] for k in order],
                  [(lbox, k) for k in order], [ln[leaving[k]] for k in order])
    for k, out in zip(order, outs):
        if rows < 16:
            out = jnp.concatenate([out, jnp.zeros((16 - rows, hd), F32)], axis=0)
        abox[k] = out.astype(BF16)
        a_copy(k).start()
    for k in order:
        p_copy(k, 1).start()
    stays(early_slots, slots)

    for k in order:
        a_copy(k).wait_recv()
    for j in range(slots):
        back = lax.rem(me - pr[j] // slots + n, n)
        got = aarr[back].astype(F32)[:rows]
        merged[pl.ds(j * rows, rows), :] = jnp.where(back == 0, att[j], got)
    for h in range(heads):
        flat[:, pl.ds(h * hd, hd)] = merged[
            pl.ds(h, slots * steps, stride=heads), :
        ].astype(BF16)
    w_copy.wait()

    def r_copy(c, i):
        return remote(pbox.at[c, lax.rem(col + i, tp)], parr.at[c, i], r_send.at[c, i],
                      r_recv.at[c, i], {"tp": lax.rem(col + i, tp)})

    for c in range(chunks):
        prod = jnp.dot(flat[...], wv[:, pl.ds(c * WIDE, WIDE)], preferred_element_type=F32)
        for d in range(tp):
            mine = prod[d * own:(d + 1) * own]
            prodf[c, d] = mine
            pbox[c, d] = jnp.concatenate(
                [mine[:, f * narrow:(f + 1) * narrow] for f in range(fold)], axis=0
            ).astype(BF16)
        for i in range(1, tp):
            r_copy(c, i).start()
    for c in range(chunks):
        total = prodf[c, col]
        for i in range(1, tp):
            r_copy(c, i).wait_recv()
            part = parr[c, i].astype(F32)
            total += jnp.concatenate(
                [part[f * own:(f + 1) * own] for f in range(fold)], axis=1
            )
        for r in range(own // steps):
            lo_ref[r, :, pl.ds(c * WIDE, WIDE)] = total[r * steps:(r + 1) * steps].astype(BF16)

    for c in range(chunks):
        for i in range(1, tp):
            r_copy(c, i).wait_send()
    for k in order:
        q_copy(k).wait_send()
        a_copy(k).wait_send()
    for j in range(slots):
        pltpu.make_async_copy(locv.at[j], loc_hbm.at[j], loc_sem.at[j]).wait()
    for k in order:
        for part in range(2):
            p_copy(k, part).wait_send()
            p_copy(k, part).wait_recv()


def place_kernel(dims, pr, nk_ref, loc_hbm, arr_hbm, lo_in, new_hbm, lo_out, vbuf, sem, in_sem):
    n, tp, slots, steps, heads, groups, pages, page, span, hd, features = dims
    body = 2 * groups * span
    me = lax.axis_index("inst")
    lo_copy = pltpu.make_async_copy(lo_in, lo_out, sem.at[slots])
    lo_copy.start()

    def source(j):
        return lax.rem(me - pr[j] // slots + n, n)

    def arrived(j):
        return pltpu.make_async_copy(arr_hbm.at[source(j)], vbuf.at[j], in_sem.at[j])

    def kept(j):
        return pltpu.make_async_copy(loc_hbm.at[j], vbuf.at[j, pl.ds(0, body)], in_sem.at[j])

    def put(j):
        return pltpu.make_async_copy(vbuf.at[j, pl.ds(0, body)], new_hbm.at[j], sem.at[j])

    for j in range(slots):
        @pl.when(source(j) != 0)
        def _():
            arrived(j).start()

        @pl.when(source(j) == 0)
        def _():
            kept(j).start()

    at = lax.broadcasted_iota(jnp.int32, (span, hd), 0)
    for j in range(slots):
        @pl.when(source(j) == 0)
        def _():
            kept(j).wait()

        @pl.when(source(j) != 0)
        def _():
            arrived(j).wait()
            known = vbuf[j, pl.ds(body, 16), :].astype(F32)[:1].astype(jnp.int32)
            for c in range(2):
                rows = [nk_ref[j, t, c].astype(F32) for t in range(steps)]
                for g in range(groups):
                    where = pl.ds((c * groups + g) * span, span)
                    x = vbuf[j, where, :].astype(F32)
                    for t in range(steps):
                        x = jnp.where(at == known + t, rows[t][g:g + 1], x)
                    vbuf[j, where, :] = x.astype(BF16)

        put(j).start()

    for j in range(slots):
        put(j).wait()
    lo_copy.wait()


def body(mesh, kv_pool, page_table, lengths, partner, queries, new_kv, out_weight):
    n, tp = mesh.shape["inst"], mesh.shape["tp"]
    slots, steps, heads, hd = queries.shape
    groups, page = kv_pool.shape[2], kv_pool.shape[3]
    pages = page_table.shape[1]
    features = out_weight.shape[1]
    span = pages * page
    dims = (n, tp, slots, steps, heads, groups, pages, page, span, hd, features)
    rows = steps * heads
    up = lambda x: -(-x // 16) * 16
    qrows = up(rows) + up(steps * 2 * groups)
    tokens = 2 * groups * span
    own = slots // tp * steps
    fold = max(1, 16 // own)
    chunks = features // WIDE
    vmem = pl.BlockSpec(memory_space=pltpu.VMEM)
    smem = pl.BlockSpec(memory_space=pltpu.SMEM)
    hbm = pl.BlockSpec(memory_space=pl.ANY)
    dma = pltpu.SemaphoreType.DMA
    loc, arr, lo = pl.pallas_call(
        functools.partial(move_kernel, dims),
        out_shape=(
            jax.ShapeDtypeStruct((slots, tokens, hd), BF16),
            jax.ShapeDtypeStruct((n, tokens + 16, hd), BF16),
            jax.ShapeDtypeStruct((slots // tp, steps, features), BF16),
        ),
        in_specs=[hbm] * 7,
        out_specs=(hbm, hbm, vmem),
        scratch_shapes=[
            pltpu.SMEM((pages, slots), jnp.int32),
            pltpu.SMEM((slots,), jnp.int32),
            pltpu.SMEM((slots,), jnp.int32),
            pltpu.VMEM(queries.shape, BF16),
            pltpu.VMEM(new_kv.shape, BF16),
            pltpu.VMEM(kv_pool.shape, BF16),
            pltpu.VMEM(out_weight.shape, BF16),
            pltpu.VMEM((slots, qrows, hd), BF16),
            pltpu.VMEM((n, qrows, hd), BF16),
            pltpu.VMEM((n, qrows, hd), BF16),
            pltpu.VMEM((n, tokens + 16, hd), BF16),
            pltpu.VMEM((n, tokens, hd), BF16),
            pltpu.VMEM((slots, tokens, hd), BF16),
            pltpu.VMEM((slots, rows, hd), F32),
            pltpu.VMEM((n, up(rows), hd), BF16),
            pltpu.VMEM((n, up(rows), hd), BF16),
            pltpu.VMEM((slots * rows, hd), F32),
            pltpu.VMEM((slots * steps, heads * hd), BF16),
            pltpu.VMEM((chunks, tp, own, WIDE), F32),
            pltpu.VMEM((chunks, tp, own * fold, WIDE // fold), BF16),
            pltpu.VMEM((chunks, tp, own * fold, WIDE // fold), BF16),
            dma((7,)), dma((slots,)),
            dma((n,)), dma((n,)), dma((n, 2)), dma((n, 2)), dma((n,)), dma((n,)),
            dma((chunks, tp)), dma((chunks, tp)),
        ],
        compiler_params=pltpu.CompilerParams(
            collective_id=0, has_side_effects=True, vmem_limit_bytes=60 << 20
        ),
        name="move",
    )(page_table.T, lengths, partner, queries, new_kv, kv_pool, out_weight)
    new_cache, layer_out = pl.pallas_call(
        functools.partial(place_kernel, dims),
        out_shape=(
            jax.ShapeDtypeStruct((slots, tokens, hd), BF16),
            jax.ShapeDtypeStruct(lo.shape, BF16),
        ),
        in_specs=[smem, vmem, hbm, hbm, hbm],
        out_specs=(hbm, hbm),
        scratch_shapes=[
            pltpu.VMEM((slots, tokens + 16, hd), BF16),
            dma((slots + 1,)), dma((slots,)),
        ],
        compiler_params=pltpu.CompilerParams(vmem_limit_bytes=60 << 20),
        name="place",
    )(partner, new_kv, loc, arr, lo)
    return layer_out, new_cache.reshape(slots, 2, groups, span, hd)


def solution(mesh):
    in_specs = (
        P(("groups", "inst"), None, "tp", None, None),
        P(("groups", "inst"), None),
        P(("groups", "inst")),
        P(("groups", "inst")),
        P(("groups", "inst"), None, "tp", None),
        P(("groups", "inst"), None, None, "tp", None),
        P("tp", None),
    )
    out_specs = (
        P(("groups", "inst", "tp"), None, None),
        P(("groups", "inst"), None, "tp", None, None),
    )
    return jax.shard_map(
        functools.partial(body, mesh), mesh=mesh, in_specs=in_specs, out_specs=out_specs,
        check_vma=False,
    )
```

```python
import functools

import jax
import jax.numpy as jnp
from jax import lax
from jax.experimental import pallas as pl
from jax.experimental.pallas import tpu as pltpu
from jax.sharding import PartitionSpec as P

MESH = pl.DeviceIdType.MESH
BF16 = jnp.bfloat16
F32 = jnp.float32
FIRST = 4
CH = 2
EARLY = 4


def width(features, fold):
    parts = CH
    while features % parts or features // parts % (128 * fold):
        parts += 1
    return features // parts


def move_kernel(
    dims, pt_hbm, ln_hbm, pr_hbm, q_hbm, nk_hbm, pool_hbm, w_hbm, loc_hbm, arr_hbm, lo_ref,
    pt, ln, pr, q_ref, nk_ref, poolv, wv, qn, qbox, qarr, obox, lbox, locv, att, abox, aarr, merged, flat, prodf, pbox, parr,
    dma_sem, loc_sem, q_send, q_recv, p_send, p_recv, a_send, a_recv, r_send, r_recv,
):
    n, tp, slots, steps, heads, groups, pages, page, span, hd, features = dims
    rows = steps * heads
    new_at = -(-rows // 16) * 16
    per = heads // groups
    body = 2 * groups * span
    me = lax.axis_index("inst")
    col = lax.axis_index("tp")
    own = slots // tp * steps
    fold = max(1, 16 // own)
    wide = width(features, fold)
    narrow = wide // fold
    chunks = features // wide

    early = [
        pltpu.make_async_copy(src, dst, dma_sem.at[at])
        for at, (src, dst) in enumerate(
            [(pr_hbm, pr), (q_hbm, q_ref), (nk_hbm, nk_ref), (pt_hbm, pt), (ln_hbm, ln)]
        )
    ]
    for copy in early:
        copy.start()
    pool_copy = pltpu.make_async_copy(pool_hbm, poolv, dma_sem.at[5])
    pool_copy.start()
    w_copy = pltpu.make_async_copy(w_hbm, wv, dma_sem.at[6])

    barrier = pltpu.get_barrier_semaphore()
    for k in range(1, n):
        pl.semaphore_signal(
            barrier, inc=1, device_id={"inst": lax.rem(me + k, n)}, device_id_type=MESH
        )
    for i in range(1, tp):
        pl.semaphore_signal(
            barrier, inc=1, device_id={"tp": lax.rem(col + i, tp)}, device_id_type=MESH
        )

    for copy in early:
        copy.wait()
    aarr[0] = jnp.zeros(aarr.shape[1:], BF16)

    def slot_for(k):
        other = lax.rem(me + k, n)
        found = jnp.int32(0)
        for j in range(slots):
            found = jnp.where(pr[j] // slots == other, jnp.int32(j), found)
        return found

    def pack(j):
        parts = [q_ref[j, t].astype(F32) for t in range(steps)]
        if new_at > rows:
            parts.append(jnp.zeros((new_at - rows, hd), F32))
        parts += [nk_ref[j, t, c].astype(F32) for t in range(steps) for c in range(2)]
        fill = qn.shape[1] - new_at - steps * 2 * groups
        parts.append(jnp.zeros((fill, hd), F32))
        return jnp.concatenate(parts, axis=0).astype(BF16)

    order = sorted(range(1, n), key=lambda k: abs(k - n // 2))
    leaving = {k: slot_for(k) for k in order}
    for k in order:
        qbox[k] = pack(leaving[k])

    def remote(src, dst, send, recv, where):
        return pltpu.make_async_remote_copy(
            src_ref=src, dst_ref=dst, send_sem=send, recv_sem=recv,
            device_id=where, device_id_type=MESH,
        )

    def q_copy(k):
        return remote(qbox.at[k], qarr.at[k], q_send.at[k], q_recv.at[k],
                      {"inst": lax.rem(me + k, n)})

    cut = (body + 16) // FIRST // 16 * 16

    def p_copy(k, part):
        at = pl.ds(0, cut) if part == 0 else pl.ds(cut, body + 16 - cut)
        return remote(obox.at[k, at], arr_hbm.at[k, at], p_send.at[k, part],
                      p_recv.at[k, part], {"inst": lax.rem(me + k, n)})

    def a_copy(k):
        return remote(abox.at[k], aarr.at[k], a_send.at[k], a_recv.at[k],
                      {"inst": lax.rem(me + k, n)})

    row_at = lax.broadcasted_iota(jnp.int32, (page, hd), 0)

    def stored(slot, known):
        for m in range(pages):
            at = row_at + page * m
            inside = at < known
            where = pt[m, slot]
            for c in range(2):
                for g in range(groups):
                    x = poolv[where, c, g].astype(F32)
                    yield m, c, g, at, jnp.where(inside, x, 0.0)

    def place(m, c, g):
        return pl.ds((c * groups + g) * span + page * m, page)

    pl.semaphore_wait(barrier, n - 1 + tp - 1)
    for k in order:
        q_copy(k).start()
    pool_copy.wait()
    w_copy.start()
    for k in order:
        known = ln[leaving[k]]
        for m, c, g, _, x in stored(leaving[k], known):
            obox[k, place(m, c, g), :] = x.astype(BF16)
        obox[k, pl.ds(body, 16), :] = jnp.full((16, hd), known.astype(F32), F32).astype(BF16)
        p_copy(k, 0).start()

    r_at = lax.broadcasted_iota(jnp.int32, (rows, groups * span), 0)
    c_at = lax.broadcasted_iota(jnp.int32, (rows, groups * span), 1)
    same = (r_at % heads) // per == c_at // span
    ahead = c_at % span - r_at // heads
    reach = jnp.where(same, ahead, span * 2)
    half = groups * span

    def finish(slot, packed, dst, j):
        known = ln[slot]
        new = packed[new_at:].astype(F32)
        for m, c, g, at, x in stored(slot, known):
            for t in range(steps):
                r = (t * 2 + c) * groups + g
                x = jnp.where(at == known + t, new[r:r + 1], x)
            dst[j, place(m, c, g), :] = x.astype(BF16)

    def attend(asked, kept, knowns):
        scores = [
            jnp.where(
                reach <= known,
                lax.dot_general(
                    q, ref[at, pl.ds(0, half), :], (((1,), (1,)), ((), ())),
                    preferred_element_type=F32,
                ) * (hd ** -0.5),
                -1e30,
            )
            for q, (ref, at), known in zip(asked, kept, knowns)
        ]
        scores = jnp.concatenate(scores, axis=0)
        expo = jnp.exp(scores - jnp.max(scores, axis=-1, keepdims=True))
        weights = expo / jnp.sum(expo, axis=-1, keepdims=True)
        return [
            jnp.dot(weights[i * rows:(i + 1) * rows].astype(BF16),
                    ref[at, pl.ds(half, half), :], preferred_element_type=F32)
            for i, (ref, at) in enumerate(kept)
        ]

    def stays(low, high):
        def one(j, carry):
            packed = pack(j)
            qn[j] = packed
            finish(pr[j] % slots, packed, locv, j)
            pltpu.make_async_copy(locv.at[j], loc_hbm.at[j], loc_sem.at[j]).start()
            return carry

        lax.fori_loop(low, high, one, 0, unroll=2)
        js = range(low, high)
        outs = attend([qn[j, pl.ds(0, new_at), :][:rows] for j in js], [(locv, j) for j in js],
                      [ln[pr[j] % slots] for j in js])
        for j, out in zip(js, outs):
            att[j] = out

    early_slots = slots // EARLY if EARLY else 0
    if early_slots:
        stays(0, early_slots)
    for k in order:
        q_copy(n - k).wait_recv()
        finish(leaving[k], qarr[n - k], lbox, k)
    outs = attend([qarr[n - k, pl.ds(0, new_at), :][:rows] for k in order],
                  [(lbox, k) for k in order], [ln[leaving[k]] for k in order])
    for k, out in zip(order, outs):
        if rows < 16:
            out = jnp.concatenate([out, jnp.zeros((16 - rows, hd), F32)], axis=0)
        abox[k] = out.astype(BF16)
        a_copy(k).start()
    for k in order:
        p_copy(k, 1).start()
    stays(early_slots, slots)

    for k in order:
        a_copy(k).wait_recv()
    for j in range(slots):
        back = lax.rem(me - pr[j] // slots + n, n)
        got = aarr[back].astype(F32)[:rows]
        merged[pl.ds(j * rows, rows), :] = jnp.where(back == 0, att[j], got)
    for h in range(heads):
        flat[:, pl.ds(h * hd, hd)] = merged[
            pl.ds(h, slots * steps, stride=heads), :
        ].astype(BF16)
    w_copy.wait()

    def r_copy(c, i):
        return remote(pbox.at[c, lax.rem(col + i, tp)], parr.at[c, i], r_send.at[c, i],
                      r_recv.at[c, i], {"tp": lax.rem(col + i, tp)})

    for c in range(chunks):
        prod = jnp.dot(flat[...], wv[:, pl.ds(c * wide, wide)], preferred_element_type=F32)
        for d in range(tp):
            mine = prod[d * own:(d + 1) * own]
            prodf[c, d] = mine
            pbox[c, d] = jnp.concatenate(
                [mine[:, f * narrow:(f + 1) * narrow] for f in range(fold)], axis=0
            ).astype(BF16)
        for i in range(1, tp):
            r_copy(c, i).start()
    for c in range(chunks):
        total = prodf[c, col]
        for i in range(1, tp):
            r_copy(c, i).wait_recv()
            part = parr[c, i].astype(F32)
            total += jnp.concatenate(
                [part[f * own:(f + 1) * own] for f in range(fold)], axis=1
            )
        for r in range(own // steps):
            lo_ref[r, :, pl.ds(c * wide, wide)] = total[r * steps:(r + 1) * steps].astype(BF16)

    for c in range(chunks):
        for i in range(1, tp):
            r_copy(c, i).wait_send()
    for k in order:
        q_copy(k).wait_send()
        a_copy(k).wait_send()
    for j in range(slots):
        pltpu.make_async_copy(locv.at[j], loc_hbm.at[j], loc_sem.at[j]).wait()
    for k in order:
        for part in range(2):
            p_copy(k, part).wait_send()
            p_copy(k, part).wait_recv()


def place_kernel(
    dims, pr_hbm, nk_hbm, loc_hbm, arr_hbm, lo_in, new_hbm, lo_out,
    pr, nk_ref, vbuf, abuf, small_sem, put_sem, loc_sem, arr_sem,
):
    n, tp, slots, steps, heads, groups, pages, page, span, hd, features = dims
    body = 2 * groups * span
    me = lax.axis_index("inst")
    pr_copy = pltpu.make_async_copy(pr_hbm, pr, small_sem.at[0])
    nk_copy = pltpu.make_async_copy(nk_hbm, nk_ref, small_sem.at[1])
    lo_copy = pltpu.make_async_copy(lo_in, lo_out, small_sem.at[2])

    def arrived(k):
        return pltpu.make_async_copy(arr_hbm.at[k], abuf.at[k], arr_sem.at[k])

    def kept(j):
        return pltpu.make_async_copy(loc_hbm.at[j], vbuf.at[j], loc_sem.at[j])

    pr_copy.start()
    for k in range(1, n):
        arrived(k).start()
    nk_copy.start()
    for j in range(slots):
        kept(j).start()
    lo_copy.start()
    pr_copy.wait()
    source = [lax.rem(me - pr[j] // slots + n, n) for j in range(slots)]

    def put(j, src):
        return pltpu.make_async_copy(src, new_hbm.at[j], put_sem.at[j])

    for k in range(1, n):
        arrived(k).wait()
    nk_copy.wait()
    at = lax.broadcasted_iota(jnp.int32, (span, hd), 0)
    for j in range(slots):
        @pl.when(source[j] != 0)
        def _():
            k = source[j]
            known = abuf[k, pl.ds(body, 16), :].astype(F32)[:1].astype(jnp.int32)
            for c in range(2):
                rows = [nk_ref[j, t, c].astype(F32) for t in range(steps)]
                for g in range(groups):
                    where = pl.ds((c * groups + g) * span, span)
                    x = abuf[k, where, :].astype(F32)
                    for t in range(steps):
                        x = jnp.where(at == known + t, rows[t][g:g + 1], x)
                    abuf[k, where, :] = x.astype(BF16)
            put(j, abuf.at[k, pl.ds(0, body)]).start()

    for j in range(slots):
        kept(j).wait()

        @pl.when(source[j] == 0)
        def _():
            put(j, vbuf.at[j]).start()

    for j in range(slots):
        put(j, vbuf.at[j]).wait()
    lo_copy.wait()


def body(mesh, kv_pool, page_table, lengths, partner, queries, new_kv, out_weight):
    n, tp = mesh.shape["inst"], mesh.shape["tp"]
    slots, steps, heads, hd = queries.shape
    groups, page = kv_pool.shape[2], kv_pool.shape[3]
    pages = page_table.shape[1]
    features = out_weight.shape[1]
    span = pages * page
    dims = (n, tp, slots, steps, heads, groups, pages, page, span, hd, features)
    rows = steps * heads
    up = lambda x: -(-x // 16) * 16
    qrows = up(rows) + up(steps * 2 * groups)
    tokens = 2 * groups * span
    own = slots // tp * steps
    fold = max(1, 16 // own)
    wide = width(features, fold)
    chunks = features // wide
    vmem = pl.BlockSpec(memory_space=pltpu.VMEM)
    hbm = pl.BlockSpec(memory_space=pl.ANY)
    dma = pltpu.SemaphoreType.DMA
    loc, arr, lo = pl.pallas_call(
        functools.partial(move_kernel, dims),
        out_shape=(
            jax.ShapeDtypeStruct((slots, tokens, hd), BF16),
            jax.ShapeDtypeStruct((n, tokens + 16, hd), BF16),
            jax.ShapeDtypeStruct((slots // tp, steps, features), BF16),
        ),
        in_specs=[hbm] * 7,
        out_specs=(hbm, hbm, vmem),
        scratch_shapes=[
            pltpu.SMEM((pages, slots), jnp.int32),
            pltpu.SMEM((slots,), jnp.int32),
            pltpu.SMEM((slots,), jnp.int32),
            pltpu.VMEM(queries.shape, BF16),
            pltpu.VMEM(new_kv.shape, BF16),
            pltpu.VMEM(kv_pool.shape, BF16),
            pltpu.VMEM(out_weight.shape, BF16),
            pltpu.VMEM((slots, qrows, hd), BF16),
            pltpu.VMEM((n, qrows, hd), BF16),
            pltpu.VMEM((n, qrows, hd), BF16),
            pltpu.VMEM((n, tokens + 16, hd), BF16),
            pltpu.VMEM((n, tokens, hd), BF16),
            pltpu.VMEM((slots, tokens, hd), BF16),
            pltpu.VMEM((slots, rows, hd), F32),
            pltpu.VMEM((n, up(rows), hd), BF16),
            pltpu.VMEM((n, up(rows), hd), BF16),
            pltpu.VMEM((slots * rows, hd), F32),
            pltpu.VMEM((slots * steps, heads * hd), BF16),
            pltpu.VMEM((chunks, tp, own, wide), F32),
            pltpu.VMEM((chunks, tp, own * fold, wide // fold), BF16),
            pltpu.VMEM((chunks, tp, own * fold, wide // fold), BF16),
            dma((7,)), dma((slots,)),
            dma((n,)), dma((n,)), dma((n, 2)), dma((n, 2)), dma((n,)), dma((n,)),
            dma((chunks, tp)), dma((chunks, tp)),
        ],
        compiler_params=pltpu.CompilerParams(
            collective_id=0, has_side_effects=True, vmem_limit_bytes=60 << 20
        ),
        name="move",
    )(page_table.T, lengths, partner, queries, new_kv, kv_pool, out_weight)
    new_cache, layer_out = pl.pallas_call(
        functools.partial(place_kernel, dims),
        out_shape=(
            jax.ShapeDtypeStruct((slots, tokens, hd), BF16),
            jax.ShapeDtypeStruct(lo.shape, BF16),
        ),
        in_specs=[hbm] * 5,
        out_specs=(hbm, hbm),
        scratch_shapes=[
            pltpu.SMEM((slots,), jnp.int32),
            pltpu.VMEM(new_kv.shape, BF16),
            pltpu.VMEM((slots, tokens, hd), BF16),
            pltpu.VMEM((n, tokens + 16, hd), BF16),
            dma((3,)), dma((slots,)), dma((slots,)), dma((n,)),
        ],
        compiler_params=pltpu.CompilerParams(vmem_limit_bytes=60 << 20),
        name="place",
    )(partner, new_kv, loc, arr, lo)
    return layer_out, new_cache.reshape(slots, 2, groups, span, hd)


def solution(mesh):
    in_specs = (
        P(("groups", "inst"), None, "tp", None, None),
        P(("groups", "inst"), None),
        P(("groups", "inst")),
        P(("groups", "inst")),
        P(("groups", "inst"), None, "tp", None),
        P(("groups", "inst"), None, None, "tp", None),
        P("tp", None),
    )
    out_specs = (
        P(("groups", "inst", "tp"), None, None),
        P(("groups", "inst"), None, "tp", None, None),
    )
    return jax.shard_map(
        functools.partial(body, mesh), mesh=mesh, in_specs=in_specs, out_specs=out_specs,
        check_vma=False,
    )
```

```python
import functools

import jax
import jax.numpy as jnp
from jax import lax
from jax.experimental import pallas as pl
from jax.experimental.pallas import tpu as pltpu
from jax.sharding import PartitionSpec as P

MESH = pl.DeviceIdType.MESH
BF16 = jnp.bfloat16
F32 = jnp.float32
FIRST = 4
CH = 2
EARLY = 4


def width(features, fold):
    parts = CH
    while features % parts or features // parts % (128 * fold):
        parts += 1
    return features // parts


def move_kernel(
    dims, pt_hbm, ln_hbm, pr_hbm, q_hbm, nk_hbm, pool_hbm, w_hbm, loc_hbm, arr_hbm, lo_ref,
    pt, ln, pr, q_ref, nk_ref, poolv, wv, qn, qbox, qarr, obox, lbox, locv, att, abox, aarr, merged, flat, prodf, pbox, parr,
    dma_sem, loc_sem, q_send, q_recv, p_send, p_recv, a_send, a_recv, r_send, r_recv,
):
    n, tp, slots, steps, heads, groups, pages, page, span, hd, features = dims
    rows = steps * heads
    new_at = -(-rows // 16) * 16
    per = heads // groups
    body = 2 * groups * span
    me = lax.axis_index("inst")
    col = lax.axis_index("tp")
    own = slots // tp * steps
    fold = max(1, 16 // own)
    wide = width(features, fold)
    narrow = wide // fold
    chunks = features // wide

    early = [
        pltpu.make_async_copy(src, dst, dma_sem.at[at])
        for at, (src, dst) in enumerate(
            [(pr_hbm, pr), (q_hbm, q_ref), (nk_hbm, nk_ref), (pt_hbm, pt), (ln_hbm, ln)]
        )
    ]
    for copy in early:
        copy.start()
    pool_copy = pltpu.make_async_copy(pool_hbm, poolv, dma_sem.at[5])
    pool_copy.start()
    w_copy = pltpu.make_async_copy(w_hbm, wv, dma_sem.at[6])

    barrier = pltpu.get_barrier_semaphore()
    for k in range(1, n):
        pl.semaphore_signal(
            barrier, inc=1, device_id={"inst": lax.rem(me + k, n)}, device_id_type=MESH
        )
    for i in range(1, tp):
        pl.semaphore_signal(
            barrier, inc=1, device_id={"tp": lax.rem(col + i, tp)}, device_id_type=MESH
        )

    for copy in early:
        copy.wait()
    aarr[0] = jnp.zeros(aarr.shape[1:], BF16)

    def slot_for(k):
        other = lax.rem(me + k, n)
        found = jnp.int32(0)
        for j in range(slots):
            found = jnp.where(pr[j] // slots == other, jnp.int32(j), found)
        return found

    def pack(j):
        parts = [q_ref[j, t].astype(F32) for t in range(steps)]
        if new_at > rows:
            parts.append(jnp.zeros((new_at - rows, hd), F32))
        parts += [nk_ref[j, t, c].astype(F32) for t in range(steps) for c in range(2)]
        fill = qn.shape[1] - new_at - steps * 2 * groups
        parts.append(jnp.zeros((fill, hd), F32))
        return jnp.concatenate(parts, axis=0).astype(BF16)

    order = sorted(range(1, n), key=lambda k: (abs(k - n // 2), -k))
    leaving = {k: slot_for(k) for k in order}
    for k in order:
        qbox[k] = pack(leaving[k])

    def remote(src, dst, send, recv, where):
        return pltpu.make_async_remote_copy(
            src_ref=src, dst_ref=dst, send_sem=send, recv_sem=recv,
            device_id=where, device_id_type=MESH,
        )

    def q_copy(k):
        return remote(qbox.at[k], qarr.at[k], q_send.at[k], q_recv.at[k],
                      {"inst": lax.rem(me + k, n)})

    cut = (body + 16) // FIRST // 16 * 16

    def p_copy(k, part):
        at = pl.ds(0, cut) if part == 0 else pl.ds(cut, body + 16 - cut)
        return remote(obox.at[k, at], arr_hbm.at[k, at], p_send.at[k, part],
                      p_recv.at[k, part], {"inst": lax.rem(me + k, n)})

    def a_copy(k):
        return remote(abox.at[k], aarr.at[k], a_send.at[k], a_recv.at[k],
                      {"inst": lax.rem(me + k, n)})

    row_at = lax.broadcasted_iota(jnp.int32, (page, hd), 0)

    def stored(slot, known):
        for m in range(pages):
            at = row_at + page * m
            inside = at < known
            where = pt[m, slot]
            for c in range(2):
                for g in range(groups):
                    x = poolv[where, c, g].astype(F32)
                    yield m, c, g, at, jnp.where(inside, x, 0.0)

    def place(m, c, g):
        return pl.ds((c * groups + g) * span + page * m, page)

    pl.semaphore_wait(barrier, n - 1 + tp - 1)
    for k in order:
        q_copy(k).start()
    pool_copy.wait()
    w_copy.start()
    for k in order:
        known = ln[leaving[k]]
        for m, c, g, _, x in stored(leaving[k], known):
            obox[k, place(m, c, g), :] = x.astype(BF16)
        obox[k, pl.ds(body, 16), :] = jnp.full((16, hd), known.astype(F32), F32).astype(BF16)
        p_copy(k, 0).start()

    r_at = lax.broadcasted_iota(jnp.int32, (rows, groups * span), 0)
    c_at = lax.broadcasted_iota(jnp.int32, (rows, groups * span), 1)
    same = (r_at % heads) // per == c_at // span
    ahead = c_at % span - r_at // heads
    reach = jnp.where(same, ahead, span * 2)
    half = groups * span

    def finish(slot, packed, dst, j):
        known = ln[slot]
        new = packed[new_at:].astype(F32)
        for m, c, g, at, x in stored(slot, known):
            for t in range(steps):
                r = (t * 2 + c) * groups + g
                x = jnp.where(at == known + t, new[r:r + 1], x)
            dst[j, place(m, c, g), :] = x.astype(BF16)

    def attend(asked, kept, knowns):
        scores = [
            jnp.where(
                reach <= known,
                lax.dot_general(
                    q, ref[at, pl.ds(0, half), :], (((1,), (1,)), ((), ())),
                    preferred_element_type=F32,
                ) * (hd ** -0.5),
                -1e30,
            )
            for q, (ref, at), known in zip(asked, kept, knowns)
        ]
        scores = jnp.concatenate(scores, axis=0)
        expo = jnp.exp(scores - jnp.max(scores, axis=-1, keepdims=True))
        weights = expo / jnp.sum(expo, axis=-1, keepdims=True)
        return [
            jnp.dot(weights[i * rows:(i + 1) * rows].astype(BF16),
                    ref[at, pl.ds(half, half), :], preferred_element_type=F32)
            for i, (ref, at) in enumerate(kept)
        ]

    def stays(low, high):
        def one(j, carry):
            packed = pack(j)
            qn[j] = packed
            finish(pr[j] % slots, packed, locv, j)
            pltpu.make_async_copy(locv.at[j], loc_hbm.at[j], loc_sem.at[j]).start()
            return carry

        lax.fori_loop(low, high, one, 0, unroll=2)
        js = range(low, high)
        outs = attend([qn[j, pl.ds(0, new_at), :][:rows] for j in js], [(locv, j) for j in js],
                      [ln[pr[j] % slots] for j in js])
        for j, out in zip(js, outs):
            att[j] = out

    early_slots = slots // EARLY if EARLY else 0
    if early_slots:
        stays(0, early_slots)
    for k in order:
        q_copy(n - k).wait_recv()
        finish(leaving[k], qarr[n - k], lbox, k)
    outs = attend([qarr[n - k, pl.ds(0, new_at), :][:rows] for k in order],
                  [(lbox, k) for k in order], [ln[leaving[k]] for k in order])
    for k, out in zip(order, outs):
        if rows < 16:
            out = jnp.concatenate([out, jnp.zeros((16 - rows, hd), F32)], axis=0)
        abox[k] = out.astype(BF16)
        a_copy(k).start()
    for k in order:
        p_copy(k, 1).start()
    stays(early_slots, slots)

    for k in order:
        a_copy(k).wait_recv()
    for j in range(slots):
        back = lax.rem(me - pr[j] // slots + n, n)
        got = aarr[back].astype(F32)[:rows]
        merged[pl.ds(j * rows, rows), :] = jnp.where(back == 0, att[j], got)
    for h in range(heads):
        flat[:, pl.ds(h * hd, hd)] = merged[
            pl.ds(h, slots * steps, stride=heads), :
        ].astype(BF16)
    w_copy.wait()

    def r_copy(c, i):
        return remote(pbox.at[c, lax.rem(col + i, tp)], parr.at[c, i], r_send.at[c, i],
                      r_recv.at[c, i], {"tp": lax.rem(col + i, tp)})

    for c in range(chunks):
        prod = jnp.dot(flat[...], wv[:, pl.ds(c * wide, wide)], preferred_element_type=F32)
        for d in range(tp):
            mine = prod[d * own:(d + 1) * own]
            prodf[c, d] = mine
            pbox[c, d] = jnp.concatenate(
                [mine[:, f * narrow:(f + 1) * narrow] for f in range(fold)], axis=0
            ).astype(BF16)
        for i in range(1, tp):
            r_copy(c, i).start()
    for c in range(chunks):
        total = prodf[c, col]
        for i in range(1, tp):
            r_copy(c, i).wait_recv()
            part = parr[c, i].astype(F32)
            total += jnp.concatenate(
                [part[f * own:(f + 1) * own] for f in range(fold)], axis=1
            )
        for r in range(own // steps):
            lo_ref[r, :, pl.ds(c * wide, wide)] = total[r * steps:(r + 1) * steps].astype(BF16)

    for c in range(chunks):
        for i in range(1, tp):
            r_copy(c, i).wait_send()
    for k in order:
        q_copy(k).wait_send()
        a_copy(k).wait_send()
    for j in range(slots):
        pltpu.make_async_copy(locv.at[j], loc_hbm.at[j], loc_sem.at[j]).wait()
    for k in order:
        for part in range(2):
            p_copy(k, part).wait_send()
            p_copy(k, part).wait_recv()


def place_kernel(
    dims, pr_hbm, nk_hbm, loc_hbm, arr_hbm, lo_in, new_hbm, lo_out,
    pr, nk_ref, vbuf, abuf, small_sem, put_sem, loc_sem, arr_sem,
):
    n, tp, slots, steps, heads, groups, pages, page, span, hd, features = dims
    body = 2 * groups * span
    me = lax.axis_index("inst")
    pr_copy = pltpu.make_async_copy(pr_hbm, pr, small_sem.at[0])
    nk_copy = pltpu.make_async_copy(nk_hbm, nk_ref, small_sem.at[1])
    lo_copy = pltpu.make_async_copy(lo_in, lo_out, small_sem.at[2])

    def arrived(k):
        return pltpu.make_async_copy(arr_hbm.at[k], abuf.at[k], arr_sem.at[k])

    def kept(j):
        return pltpu.make_async_copy(loc_hbm.at[j], vbuf.at[j], loc_sem.at[j])

    pr_copy.start()
    for k in range(1, n):
        arrived(k).start()
    nk_copy.start()
    for j in range(slots):
        kept(j).start()
    lo_copy.start()
    pr_copy.wait()
    source = [lax.rem(me - pr[j] // slots + n, n) for j in range(slots)]

    def put(j, src):
        return pltpu.make_async_copy(src, new_hbm.at[j], put_sem.at[j])

    for k in range(1, n):
        arrived(k).wait()
    nk_copy.wait()
    at = lax.broadcasted_iota(jnp.int32, (span, hd), 0)
    for j in range(slots):
        @pl.when(source[j] != 0)
        def _():
            k = source[j]
            known = abuf[k, pl.ds(body, 16), :].astype(F32)[:1].astype(jnp.int32)
            for c in range(2):
                rows = [nk_ref[j, t, c].astype(F32) for t in range(steps)]
                for g in range(groups):
                    where = pl.ds((c * groups + g) * span, span)
                    x = abuf[k, where, :].astype(F32)
                    for t in range(steps):
                        x = jnp.where(at == known + t, rows[t][g:g + 1], x)
                    abuf[k, where, :] = x.astype(BF16)
            put(j, abuf.at[k, pl.ds(0, body)]).start()

    for j in range(slots):
        kept(j).wait()

        @pl.when(source[j] == 0)
        def _():
            put(j, vbuf.at[j]).start()

    for j in range(slots):
        put(j, vbuf.at[j]).wait()
    lo_copy.wait()


def body(mesh, kv_pool, page_table, lengths, partner, queries, new_kv, out_weight):
    n, tp = mesh.shape["inst"], mesh.shape["tp"]
    slots, steps, heads, hd = queries.shape
    groups, page = kv_pool.shape[2], kv_pool.shape[3]
    pages = page_table.shape[1]
    features = out_weight.shape[1]
    span = pages * page
    dims = (n, tp, slots, steps, heads, groups, pages, page, span, hd, features)
    rows = steps * heads
    up = lambda x: -(-x // 16) * 16
    qrows = up(rows) + up(steps * 2 * groups)
    tokens = 2 * groups * span
    own = slots // tp * steps
    fold = max(1, 16 // own)
    wide = width(features, fold)
    chunks = features // wide
    vmem = pl.BlockSpec(memory_space=pltpu.VMEM)
    hbm = pl.BlockSpec(memory_space=pl.ANY)
    dma = pltpu.SemaphoreType.DMA
    loc, arr, lo = pl.pallas_call(
        functools.partial(move_kernel, dims),
        out_shape=(
            jax.ShapeDtypeStruct((slots, tokens, hd), BF16),
            jax.ShapeDtypeStruct((n, tokens + 16, hd), BF16),
            jax.ShapeDtypeStruct((slots // tp, steps, features), BF16),
        ),
        in_specs=[hbm] * 7,
        out_specs=(hbm, hbm, vmem),
        scratch_shapes=[
            pltpu.SMEM((pages, slots), jnp.int32),
            pltpu.SMEM((slots,), jnp.int32),
            pltpu.SMEM((slots,), jnp.int32),
            pltpu.VMEM(queries.shape, BF16),
            pltpu.VMEM(new_kv.shape, BF16),
            pltpu.VMEM(kv_pool.shape, BF16),
            pltpu.VMEM(out_weight.shape, BF16),
            pltpu.VMEM((slots, qrows, hd), BF16),
            pltpu.VMEM((n, qrows, hd), BF16),
            pltpu.VMEM((n, qrows, hd), BF16),
            pltpu.VMEM((n, tokens + 16, hd), BF16),
            pltpu.VMEM((n, tokens, hd), BF16),
            pltpu.VMEM((slots, tokens, hd), BF16),
            pltpu.VMEM((slots, rows, hd), F32),
            pltpu.VMEM((n, up(rows), hd), BF16),
            pltpu.VMEM((n, up(rows), hd), BF16),
            pltpu.VMEM((slots * rows, hd), F32),
            pltpu.VMEM((slots * steps, heads * hd), BF16),
            pltpu.VMEM((chunks, tp, own, wide), F32),
            pltpu.VMEM((chunks, tp, own * fold, wide // fold), BF16),
            pltpu.VMEM((chunks, tp, own * fold, wide // fold), BF16),
            dma((7,)), dma((slots,)),
            dma((n,)), dma((n,)), dma((n, 2)), dma((n, 2)), dma((n,)), dma((n,)),
            dma((chunks, tp)), dma((chunks, tp)),
        ],
        compiler_params=pltpu.CompilerParams(
            collective_id=0, has_side_effects=True, vmem_limit_bytes=60 << 20
        ),
        name="move",
    )(page_table.T, lengths, partner, queries, new_kv, kv_pool, out_weight)
    new_cache, layer_out = pl.pallas_call(
        functools.partial(place_kernel, dims),
        out_shape=(
            jax.ShapeDtypeStruct((slots, tokens, hd), BF16),
            jax.ShapeDtypeStruct(lo.shape, BF16),
        ),
        in_specs=[hbm] * 5,
        out_specs=(hbm, hbm),
        scratch_shapes=[
            pltpu.SMEM((slots,), jnp.int32),
            pltpu.VMEM(new_kv.shape, BF16),
            pltpu.VMEM((slots, tokens, hd), BF16),
            pltpu.VMEM((n, tokens + 16, hd), BF16),
            dma((3,)), dma((slots,)), dma((slots,)), dma((n,)),
        ],
        compiler_params=pltpu.CompilerParams(vmem_limit_bytes=60 << 20),
        name="place",
    )(partner, new_kv, loc, arr, lo)
    return layer_out, new_cache.reshape(slots, 2, groups, span, hd)


def solution(mesh):
    in_specs = (
        P(("groups", "inst"), None, "tp", None, None),
        P(("groups", "inst"), None),
        P(("groups", "inst")),
        P(("groups", "inst")),
        P(("groups", "inst"), None, "tp", None),
        P(("groups", "inst"), None, None, "tp", None),
        P("tp", None),
    )
    out_specs = (
        P(("groups", "inst", "tp"), None, None),
        P(("groups", "inst"), None, "tp", None, None),
    )
    return jax.shard_map(
        functools.partial(body, mesh), mesh=mesh, in_specs=in_specs, out_specs=out_specs,
        check_vma=False,
    )
```
